512 devices in a mesh: ctx: 64 (over z, x_lo, core), hg: 8 (over y, x_hi).
Axes of the slice: x: 4 (x_hi: 2, x_lo: 2; x = x_hi * 2 + x_lo), y: 4, z: 16, core: 2. Of those that a mesh axis runs over, the one named last changes fastest.
Arguments:
- hidden_in: bfloat16 [8192, 4096], P('ctx', 'hg')
- norm_gain: bfloat16 [4096], P('hg'), may hold values from 0.3984375 to 1.59375
- w_query: bfloat16 [4096, 4096], P('ctx', 'hg')
- w_key: bfloat16 [4096, 1024], P('ctx', 'hg')
- w_value: bfloat16 [4096, 1024], P('ctx', 'hg'), may hold values from -0.09375 to 0.09375
- block_mask: int32 [64, 64], replicated, may hold values from 0 to 1, as said below
Outputs:
- context: bfloat16 [8192, 4096], P('ctx', 'hg')
The draws below stay inside these ranges and needn't reach their ends.
Inputs may be any that keep to these rules, and one draw needn't show every extreme that they name: `block_mask`: mask block b shows camera b % 8 at time b // 8; entry (i, j) is 1 only if j // 8 <= i // 8, and always where the two blocks show the same camera at such times, so the diagonal is 1.
All inputs are finite; a program needn't handle non-finite values.
Results may differ from the reference program's by a relative error of at most 0.0095.
Values may be sent and summed in bfloat16 or wider, within the bound.
A program may use at most 64 MiB of HBM per device.

```python
import jax
import jax.numpy as jnp
from jax import lax

D = 4096
HEADS = 32
KV_HEADS = 8
HEAD_DIM = 128
BLOCK = 128
CAMS = 8
TOKENS = 8192
NB = 64


def draw_w_query(key, part):
    folded = jax.random.fold_in(key, 7)
    base = jnp.clip(jax.random.normal(folded, (D, HEADS * HEAD_DIM), jnp.float32), -6.0, 6.0) * D ** (-0.5)
    return base.astype(jnp.bfloat16)


def draw_w_key(key, part):
    folded = jax.random.fold_in(key, 8)
    base = jnp.clip(jax.random.normal(folded, (D, KV_HEADS * HEAD_DIM), jnp.float32), -6.0, 6.0) * D ** (-0.5)
    return base.astype(jnp.bfloat16)


def draw_hidden_in(key, part):
    folded = jax.random.fold_in(key, 5)
    first = jax.random.fold_in(folded, 0)
    return jnp.clip(jax.random.normal(first, (TOKENS, D), jnp.float32), -6.0, 6.0).astype(jnp.bfloat16)


def draw_block_mask(key, part):
    key = jax.random.fold_in(key, 9)
    index = jnp.arange(NB)
    times = index // CAMS
    cameras = index % CAMS
    coins = jax.random.randint(key, (NB, NB), 0, 2)
    earlier = times[None, :] <= times[:, None]
    same = cameras[None, :] == cameras[:, None]
    return (earlier & (same | (coins == 1))).astype(jnp.int32)


def block_levels(own_key, extent, shards, low, largest):
    def one(axis_at, shards_of):
        steps = jax.random.uniform(jax.random.fold_in(jax.random.fold_in(own_key, 6), axis_at), (shards_of,), jnp.float32, low / len(shards), largest / len(shards))
        return jnp.repeat(jnp.exp(steps), extent[axis_at] // shards_of).reshape((-1,) + (1,) * (len(extent) - axis_at - 1))

    factor_of = one(*shards[0])
    for cut in shards[1:]:
        factor_of = factor_of * one(*cut)
    return factor_of


def bell_draw(stream_key, extent, spread, limit, cuts=(), dtype=jnp.bfloat16):
    result = jax.random.normal(stream_key, extent, jnp.float32) * spread
    if len(cuts) > 0:
        result = block_levels(stream_key, extent, cuts, -0.22, 0.18) * result
    return jnp.clip(result, min=-limit, max=limit).astype(dtype)


def setup_inputs(seed: int = 0) -> dict:
    key_list = jax.random.split(jax.random.key(seed), 7)
    hidden_in = draw_hidden_in(jax.random.fold_in(key_list[6], 71), 0)
    norm_gain = jnp.clip(1.0 + 0.12 * jax.random.normal(key_list[1], (D,), jnp.float32), 0.3984375, 1.59375).astype(jnp.bfloat16)
    w_query = draw_w_query(jax.random.fold_in(key_list[6], 71), 0)
    w_key = draw_w_key(jax.random.fold_in(key_list[6], 71), 0)
    w_value = bell_draw(key_list[4], (D, KV_HEADS * HEAD_DIM), D ** -0.5, 0.09375, ((0, 64), (1, 8)))
    block_mask = draw_block_mask(jax.random.fold_in(key_list[6], 71), 0)
    return dict(hidden_in=hidden_in, norm_gain=norm_gain, w_query=w_query, w_key=w_key, w_value=w_value, block_mask=block_mask)


rope_base = 500000.0

def rotate(field, positions):
    half = field.shape[-1] // 2
    freq = rope_base ** (-jnp.arange(0, 2 * half, 2).astype(jnp.float32) / (2 * half))
    angles = positions[:, None] * freq[None, :]
    cosine = jnp.cos(angles)[:, None, :]
    sine = jnp.sin(angles)[:, None, :]
    first = field[..., :half]
    second = field[..., half:]
    return jnp.concatenate([first * cosine - second * sine, second * cosine + first * sine], axis=-1)

def reference(hidden_in, norm_gain, w_query, w_key, w_value, block_mask):
    values = hidden_in.astype(jnp.float32)
    inverse = lax.rsqrt(lax.optimization_barrier(jnp.mean(values * values, axis=-1, keepdims=True)) + 1e-05)
    normed = (values * inverse * norm_gain.astype(jnp.float32)).astype(jnp.bfloat16)
    query = jnp.dot(normed, w_query, preferred_element_type=jnp.float32)
    key = jnp.dot(normed, w_key, preferred_element_type=jnp.float32)
    value = jnp.dot(normed, w_value, preferred_element_type=jnp.float32).astype(jnp.bfloat16)
    positions = jnp.arange(TOKENS).astype(jnp.float32)
    group = HEADS // KV_HEADS
    query_rot = rotate(query.reshape(TOKENS, HEADS, HEAD_DIM), positions).astype(jnp.bfloat16)
    key_rot = rotate(key.reshape(TOKENS, KV_HEADS, HEAD_DIM), positions).astype(jnp.bfloat16)
    value_heads = value.reshape(TOKENS, KV_HEADS, HEAD_DIM)
    key_wide = key_rot.astype(jnp.float32)
    value_wide = value_heads.astype(jnp.float32)
    rows_per = 512
    count = TOKENS // rows_per
    query_blocks = query_rot.reshape(count, rows_per, KV_HEADS, group, HEAD_DIM)
    starts = (jnp.arange(count) * rows_per).astype(jnp.int32)
    scale = HEAD_DIM ** (-0.5)

    def one_block(item):
        block_query, start = item
        mask_rows = lax.dynamic_slice_in_dim(block_mask, (start // BLOCK).astype(jnp.int32), rows_per // BLOCK, 0)
        allowed = jnp.repeat(jnp.repeat(mask_rows > 0, BLOCK, axis=0), BLOCK, axis=1)
        outputs = []
        for head in range(KV_HEADS):
            scores = jnp.einsum('qgd,kd->gqk', block_query[:, head].astype(jnp.float32), key_wide[:, head]) * scale
            masked = jnp.where(allowed[None], scores, jnp.float32(-1e+30))
            rowmax = lax.optimization_barrier(jnp.max(masked, axis=-1, keepdims=True))
            weights = jnp.where(allowed[None], jnp.exp(masked - rowmax), jnp.float32(0.0))
            total = lax.optimization_barrier(jnp.sum(weights, axis=-1))
            summed = jnp.einsum('gqk,kd->gqd', weights.astype(jnp.bfloat16).astype(jnp.float32), value_wide[:, head])
            outputs.append(summed / total[..., None])
        stacked = jnp.stack(outputs, axis=0)
        return jnp.transpose(stacked, (2, 0, 1, 3)).reshape(rows_per, HEADS * HEAD_DIM).astype(jnp.bfloat16)
    blocks = lax.map(one_block, (query_blocks, starts))
    return blocks.reshape(TOKENS, HEADS * HEAD_DIM)
```

```python
import math

import jax
import jax.numpy as jnp
from jax import lax
from jax.experimental import pallas as pl
from jax.experimental.pallas import tpu as pltpu
from jax.sharding import PartitionSpec as P

MESH = pl.DeviceIdType.MESH
BF16, F32 = jnp.bfloat16, jnp.float32
NZ, NY = 16, 4
ROWS = 128
ROPE_BASE = 500000.0
EXP_SCALE = 128 ** (-0.5) * math.log2(math.e)
BIG = 1e30
UP, DOWN = 8, 7

Z_UP, Z_DN = 0, 8
C_OWN, C_UP, C_DN = 15, 16, 24
PLAIN = 31
X_OWN, X_UP, X_DN = 31, 32, 40
CX_OWN, CX_UP, CX_DN = 47, 48, 56
FULL = 63


def kernel(
    x_ref, gain_ref, wq_ref, wk_ref, wv_ref, cos_ref, sin_ref, mask_ref, o_ref,
    xs, xbuf, nb, wkv, wq, kv, sq, pkv, pq, qt, m_ref, l_ref, acc,
    x_s, x_r, wkv_s, wkv_r, wq_s, wq_r, kv_s, kv_r, p_s, p_r,
):
    c = lax.axis_index("ctx")
    g = lax.axis_index("hg")
    z, xl, co = c // 4, (c // 2) % 2, c % 2
    y, xh = g // 2, g % 2

    def device(dz=0, flip_x=False, flip_c=False, dy=0, flip_h=False):
        zz = (z + dz + NZ) % NZ
        yy = (y + dy + NY) % NY
        a = 1 - xl if flip_x else xl
        b = 1 - co if flip_c else co
        h = 1 - xh if flip_h else xh
        return (zz * 4 + a * 2 + b, yy * 2 + h)

    up1, dn1, up2, dn2 = device(dz=1), device(dz=-1), device(dz=2), device(dz=-2)
    core, xp = device(flip_c=True), device(flip_x=True)
    hp, xx = device(flip_h=True), device(flip_x=True, flip_h=True)
    yu, yd = device(dy=1), device(dy=-1)
    peers = (up1, dn1, up2, dn2, core, xp, hp, xx, yu, yd)

    bar = pltpu.get_barrier_semaphore()
    for p in peers:
        pl.semaphore_signal(bar, inc=1, device_id=p, device_id_type=MESH)

    gain = jnp.broadcast_to(gain_ref[...].astype(F32), (16, 512)).astype(BF16)
    for q in range(2):
        for k in range(2):
            lanes = pl.ds((2 * k + q) * 128, 128)
            xs[q, pl.ds(0, ROWS), pl.ds(k * 128, 128)] = x_ref[:, lanes]
            xs[q, pl.ds(ROWS, 16), pl.ds(k * 128, 128)] = gain[:, (2 * k + q) * 128 : (2 * k + q + 1) * 128]
    xbuf[g, xl] = xs[xl]
    wkv[z, co, :, pl.ds(0, 128)] = wk_ref[...]
    wkv[z, co, :, pl.ds(128, 128)] = wv_ref[...]
    wq[z, co] = wq_ref[...]

    pl.semaphore_wait(bar, len(peers))

    started = []

    def send(src, dst, ssem, rsem, dev):
        copy = pltpu.make_async_remote_copy(
            src_ref=src, dst_ref=dst, send_sem=ssem, recv_sem=rsem,
            device_id=dev, device_id_type=MESH,
        )
        copy.start()
        started.append(copy)

    def arrive(dst, ssem, rsem):
        pltpu.make_async_remote_copy(
            src_ref=dst, dst_ref=dst, send_sem=ssem, recv_sem=rsem,
            device_id=core, device_id_type=MESH,
        ).wait_recv()

    class Stream:
        def __init__(self, slot, ssem, rsem, across):
            self.slot, self.s, self.r, self.across = slot, ssem, rsem, across

        def push(self, at, place, dev):
            ref = self.slot(*at)
            send(ref, ref, self.s.at[place], self.r.at[place], dev)

        def take(self, at, place):
            arrive(self.slot(*at), self.s.at[place], self.r.at[place])

        def own(self):
            at = (z, xl, co)
            self.push(at, Z_UP + 1, up2)
            self.push(at, Z_DN + 1, dn2)
            self.push(at, Z_UP, up1)
            self.push(at, Z_DN, dn1)
            if self.across:
                self.push(at, X_OWN, xp)
            self.push(at, C_OWN, core)

        def up(self, d):
            at = ((z - d + NZ) % NZ, xl, co)
            self.take(at, Z_UP + d - 1)
            if d % 2 == 0 and d < UP:
                self.push(at, Z_UP + d + 1, up2)
                self.push(at, Z_UP + d, up1)
            if self.across:
                self.push(at, X_UP + d - 1, xp)
            self.push(at, C_UP + d - 1, core)

        def down(self, d):
            at = ((z + d) % NZ, xl, co)
            self.take(at, Z_DN + d - 1)
            if d % 2 == 0 and d < DOWN:
                if d + 2 <= DOWN:
                    self.push(at, Z_DN + d + 1, dn2)
                self.push(at, Z_DN + d, dn1)
            if self.across:
                self.push(at, X_DN + d - 1, xp)
            self.push(at, C_DN + d - 1, core)

        def step(self, k):
            for d in (2 * k, 2 * k - 1):
                self.up(d)
                if d <= DOWN:
                    self.down(d)

        def from_core(self):
            oc = 1 - co
            self.take((z, xl, oc), C_OWN)
            for d in range(1, UP + 1):
                self.take(((z - d + NZ) % NZ, xl, oc), C_UP + d - 1)
            for d in range(1, DOWN + 1):
                self.take(((z + d) % NZ, xl, oc), C_DN + d - 1)

    kvw = Stream(lambda zz, a, b: wkv.at[zz, b], wkv_s, wkv_r, False)
    qw = Stream(lambda zz, a, b: wq.at[zz, b], wq_s, wq_r, False)
    both = Stream(lambda zz, a, b: kv.at[zz * 4 + a * 2 + b], kv_s, kv_r, True)

    pieces = ((xh, xl), (xh, 1 - xl), (1 - xh, xl), (1 - xh, 1 - xl))

    def x_push(src, i, yy, place, dev):
        h, t = pieces[i]
        send(src, xbuf.at[yy * 2 + h, t], x_s.at[place], x_r.at[place], dev)

    def x_take(i, yy, place):
        h, t = pieces[i]
        arrive(xbuf.at[yy * 2 + h, t], x_s.at[place], x_r.at[place])

    def x_held(i, yy):
        h, t = pieces[i]
        return xbuf.at[yy * 2 + h, t]

    kvw.own()
    for i, dev, part in ((1, xp, 1 - xl), (2, hp, xl), (3, xx, 1 - xl)):
        send(xs.at[part], xbuf.at[g, xl], x_s.at[i - 1], x_r.at[i - 1], dev)
    for i in range(4):
        if i > 0:
            x_take(i, y, i - 1)
        x_push(x_held(i, y), i, y, 3 + i, yu)
        x_push(x_held(i, y), i, y, 7 + i, yd)
        if i == 0:
            qw.own()
    below, above, far = (y + NY - 1) % NY, (y + 1) % NY, (y + 2) % NY

    def x_turn(i):
        x_take(i, below, 3 + i)
        if i < 2:
            x_push(x_held(i, below), i, below, 11 + i, yu)
        x_take(i, above, 7 + i)
        if i >= 2:
            x_push(x_held(i, above), i, above, 11 + i, yd)

    kvw.step(1)
    x_turn(0)
    x_turn(1)
    qw.step(1)
    kvw.step(2)
    x_turn(2)
    x_turn(3)
    qw.step(2)
    for i in range(4):
        x_take(i, far, 11 + i)

    eye = lax.broadcasted_iota(jnp.int32, (ROWS, ROWS), 0) == lax.broadcasted_iota(jnp.int32, (ROWS, ROWS), 1)
    sq[0] = jnp.zeros((8, 128), F32)
    for t in range(2):
        col = jnp.zeros((ROWS, 256), F32)
        for h in range(8):
            v = xbuf[h, t, pl.ds(0, ROWS)].astype(F32)
            col += v * v
        col = jnp.sum(col, axis=1, keepdims=True)
        sq[0, pl.ds(t, 1)] = jnp.sum(jnp.where(eye, col, 0.0), axis=0, keepdims=True)
    send(sq.at[0], sq.at[1], p_s.at[0], p_r.at[0], xp)
    kvw.step(3)
    qw.step(3)
    arrive(sq.at[1], p_s.at[0], p_r.at[0])
    for t in range(2):
        total = sq[0, pl.ds(t, 1)] + sq[1, pl.ds(t, 1)]
        inv = lax.rsqrt(total * (1.0 / 4096) + 1e-05)
        inv = jnp.sum(jnp.where(eye, inv, 0.0), axis=1, keepdims=True)
        for h in range(8):
            v = xbuf[h, t, pl.ds(0, ROWS)].astype(F32)
            scale = xbuf[h, t, pl.ds(ROWS, 16)].astype(F32)[0:1]
            nb[h, pl.ds(t * ROWS, ROWS)] = (v * inv * scale).astype(BF16)
    kvw.step(4)
    kvw.from_core()

    def project(w, cols, first):
        rows = pl.ds(first * ROWS, ROWS)
        out = jnp.zeros((ROWS, cols), F32)
        for h in range(8):
            out += jnp.dot(
                nb[h, rows], w[pl.ds(2 * h, 2)].reshape(256, cols), preferred_element_type=F32
            )
        return out

    cos, sin = cos_ref[...], sin_ref[...]

    def rotate(v):
        swapped = jnp.concatenate([v[:, 64:], v[:, :64]], axis=1)
        return v * cos + swapped * sin

    pkv[0] = project(wkv, 256, 1 - xl)
    send(pkv.at[0], pkv.at[1], p_s.at[1], p_r.at[1], xp)
    mine = project(wkv, 256, xl)
    arrive(pkv.at[1], p_s.at[1], p_r.at[1])
    mine = mine + pkv[1]
    kv[c, :, pl.ds(0, 128)] = rotate(mine[:, :128]).astype(BF16)
    kv[c, :, pl.ds(128, 128)] = mine[:, 128:].T.astype(BF16)
    both.own()
    qw.step(4)
    both.step(1)
    qw.from_core()
    pq[0] = project(wq, 512, 1 - xl)
    send(pq.at[0], pq.at[1], p_s.at[2], p_r.at[2], xp)
    pq[2] = project(wq, 512, xl)
    both.step(2)
    arrive(pq.at[1], p_s.at[2], p_r.at[2])
    for h in range(4):
        lanes = pl.ds(h * 128, 128)
        qt[:, lanes] = rotate(pq[1, :, lanes] + pq[2, :, lanes]).T.astype(BF16)

    m_ref[...] = jnp.full((1, 512), -BIG, F32)
    l_ref[...] = jnp.zeros((1, 512), F32)
    acc[...] = jnp.zeros((128, 512), F32)

    def attend(zz):
        held = kv[pl.ds(zz * 4, 4)]
        keys = held[:, :, :128].reshape(512, 128)
        vals = jnp.concatenate([held[j, :, 128:] for j in range(4)], axis=1)
        scores = jnp.dot(keys, qt[...], preferred_element_type=F32)
        old = m_ref[...]
        new = old
        shut = []
        for j in range(4):
            shut.append((1 - mask_ref[c, zz * 4 + j]).astype(F32) * BIG)
            top = jnp.max(scores[j * 128 : (j + 1) * 128], axis=0, keepdims=True)
            new = jnp.maximum(new, top * EXP_SCALE - shut[j])
        factor = jnp.exp2(old - new)
        total = l_ref[...] * factor
        parts = []
        for j in range(4):
            w = jnp.exp2(scores[j * 128 : (j + 1) * 128] * EXP_SCALE - (new + shut[j]))
            total = total + jnp.sum(w, axis=0, keepdims=True)
            parts.append(w.astype(BF16))
        m_ref[...] = new
        l_ref[...] = total
        acc[...] = acc[...] * factor + jnp.dot(
            vals, jnp.concatenate(parts, axis=0), preferred_element_type=F32
        )

    oc, ox = 1 - co, 1 - xl

    def cross(at, x_place, cx_place):
        both.take((at, ox, co), x_place)
        both.push((at, ox, co), cx_place, core)

    def gather_rest(at, c_place, cx_place):
        both.take((at, xl, oc), c_place)
        both.take((at, ox, oc), cx_place)

    cross(z, X_OWN, CX_OWN)
    gather_rest(z, C_OWN, CX_OWN)
    attend(z)
    both.step(3)
    ups = lambda d: (z - d + NZ) % NZ
    dns = lambda d: (z + d) % NZ

    def crosses(k):
        for d in (2 * k, 2 * k - 1):
            cross(ups(d), X_UP + d - 1, CX_UP + d - 1)
            if d <= DOWN:
                cross(dns(d), X_DN + d - 1, CX_DN + d - 1)

    def attends(k):
        for d in (2 * k, 2 * k - 1):
            gather_rest(ups(d), C_UP + d - 1, CX_UP + d - 1)
            attend(ups(d))
            if d <= DOWN:
                gather_rest(dns(d), C_DN + d - 1, CX_DN + d - 1)
                attend(dns(d))

    crosses(1)
    attends(1)
    both.step(4)
    for k in (2, 3, 4):
        crosses(k)
        attends(k)

    inverse = 1.0 / l_ref[...]
    for h in range(4):
        lanes = pl.ds(h * 128, 128)
        o_ref[:, lanes] = (acc[:, lanes] * inverse[:, h * 128 : (h + 1) * 128]).T.astype(BF16)
    for copy in started:
        copy.wait_send()


def shards(hidden_in, norm_gain, w_query, w_key, w_value, block_mask):
    positions = (lax.axis_index("ctx") * ROWS + jnp.arange(ROWS)).astype(F32)
    freq = ROPE_BASE ** (-jnp.arange(0, 128, 2).astype(F32) / 128)
    angles = positions[:, None] * freq[None, :]
    cosine, sine = jnp.cos(angles), jnp.sin(angles)
    cos = jnp.concatenate([cosine, cosine], axis=1)
    sin = jnp.concatenate([-sine, sine], axis=1)
    vmem = pl.BlockSpec(memory_space=pltpu.VMEM)
    dma = pltpu.SemaphoreType.DMA
    return pl.pallas_call(
        kernel,
        out_shape=jax.ShapeDtypeStruct((ROWS, 512), BF16),
        in_specs=[vmem] * 7 + [pl.BlockSpec(memory_space=pltpu.SMEM)],
        out_specs=vmem,
        scratch_shapes=[
            pltpu.VMEM((2, ROWS + 16, 256), BF16),
            pltpu.VMEM((8, 2, ROWS + 16, 256), BF16),
            pltpu.VMEM((8, 2 * ROWS, 256), BF16),
            pltpu.VMEM((NZ, 2, 64, 256), BF16),
            pltpu.VMEM((NZ, 2, 64, 512), BF16),
            pltpu.VMEM((64, ROWS, 256), BF16),
            pltpu.VMEM((2, 8, 128), F32),
            pltpu.VMEM((2, ROWS, 256), F32),
            pltpu.VMEM((3, ROWS, 512), F32),
            pltpu.VMEM((128, 512), BF16),
            pltpu.VMEM((1, 512), F32),
            pltpu.VMEM((1, 512), F32),
            pltpu.VMEM((128, 512), F32),
            dma((15,)), dma((15,)),
            dma((PLAIN,)), dma((PLAIN,)),
            dma((PLAIN,)), dma((PLAIN,)),
            dma((FULL,)), dma((FULL,)),
            dma((3,)), dma((3,)),
        ],
        compiler_params=pltpu.CompilerParams(
            collective_id=0, has_side_effects=True, vmem_limit_bytes=48 * 2**20
        ),
        cost_estimate=pl.CostEstimate(flops=3 * 10**9, bytes_accessed=2**20, transcendentals=4 * 2**20),
    )(hidden_in, norm_gain.reshape(1, 512), w_query, w_key, w_value, cos, sin, block_mask)


def solution(mesh):
    placed = (P("ctx", "hg"), P("hg"), P("ctx", "hg"), P("ctx", "hg"), P("ctx", "hg"), P())
    return jax.shard_map(
        shards, mesh=mesh, in_specs=placed, out_specs=P("ctx", "hg"), check_vma=False
    )
```
